32 devices in a mesh: tensor: 4 (over y, x), dp: 2 (over core), context: 4 (over z).
Axes of the slice: x: 2, y: 2, z: 4, core: 2. Of those that a mesh axis runs over, the one named last changes fastest.
Arguments:
- tokens: bfloat16 [2048, 4, 768], P('context', 'dp'), may hold values from -6 to 6
- segments: int32 [2048, 4], P(None, 'dp'), may hold values from 0 to 1, as said below
- ln1_gain: float32 [768], replicated, may hold values from 0.5 to 1.5
- ln1_bias: float32 [768], replicated, may hold values from -1 to 1
- qkv_weight: bfloat16 [768, 3, 768], P(None, None, 'tensor'), may hold values from -0.21875 to 0.21875
- qv_bias: float32 [2, 768], P(None, 'tensor'), may hold values from -1 to 1
- out_weight: bfloat16 [768, 768], P('tensor'), may hold values from -1.75 to 1.75
- out_bias: float32 [768], replicated, may hold values from -1 to 1
- ln2_gain: float32 [768], replicated, may hold values from 0.5 to 1.5
- ln2_bias: float32 [768], replicated, may hold values from -1 to 1
- fc1_weight: bfloat16 [768, 3072], P(None, 'tensor'), may hold values from -0.21875 to 0.21875
- fc1_bias: float32 [3072], P('tensor'), may hold values from -1 to 1
- fc2_weight: bfloat16 [3072, 768], P('tensor'), may hold values from -0.109375 to 0.109375
- fc2_bias: float32 [768], replicated, may hold values from -1 to 1
- cotangent: bfloat16 [2048, 4, 768], P('context', 'dp'), may hold values from -6 to 6
Outputs:
- output: bfloat16 [2048, 4, 768], P('context', 'dp')
- grad_tokens: float32 [2048, 4, 768], P('context', 'dp')
- ln1_gain_grad: float32 [768], replicated
- ln1_bias_grad: float32 [768], replicated
- qkv_weight_grad: float32 [768, 3, 768], P(None, None, 'tensor')
- qv_bias_grad: float32 [2, 768], P(None, 'tensor')
- out_weight_grad: float32 [768, 768], P('tensor')
- out_bias_grad: float32 [768], replicated
- ln2_gain_grad: float32 [768], replicated
- ln2_bias_grad: float32 [768], replicated
- fc1_weight_grad: float32 [768, 3072], P(None, 'tensor')
- fc1_bias_grad: float32 [3072], P('tensor')
- fc2_weight_grad: float32 [3072, 768], P('tensor')
- fc2_bias_grad: float32 [768], replicated
The draws below stay inside these ranges and needn't reach their ends.
Inputs may be any that keep to these rules, and one draw needn't show every extreme that they name: `segments`: along each sequence the document number starts at 0 and rises by 0 or 1 from one token to the next. In each aligned block of 2 sequences one, chosen by the seed, is a single document of 2048 tokens; every other sequence holds exactly max(2, 2) documents.
All inputs are finite; a program needn't handle non-finite values.
Results may differ from the reference program's by a relative error of at most 0.019.
Values may be sent and summed in bfloat16 or wider, within the bound.
A program may use at most 128 MiB of HBM per device.

```python
import math
import jax
import jax.numpy as jnp
from jax import lax

D = 768
HEAD_DIM = 64
FF = 3072
SEQS_DEV = 2
SEQ_LEN = 2048
SEQS = 4


def draw_segments(key, part):
    key = jax.random.fold_in(key, 7)
    weight_key, pick_key = jax.random.split(key)
    doc_count = max(2, SEQ_LEN // 1024)
    least = SEQ_LEN // (2 * doc_count)
    spare = SEQ_LEN - doc_count * least
    shares = jax.random.randint(weight_key, (SEQS, doc_count), 1, 101)
    totals = jnp.sum(shares, axis=1, keepdims=True)
    extra = spare * shares // totals
    extra = extra.at[:, doc_count - 1].add(spare - jnp.sum(extra, axis=1))
    doc_lengths = least + extra
    doc_ends = jnp.cumsum(doc_lengths, axis=1)
    positions = jnp.arange(SEQ_LEN, dtype=jnp.int32)
    numbers = jnp.sum((doc_ends[:, None, :] <= positions[None, :, None]).astype(jnp.int32), axis=-1)
    numbers = jnp.minimum(numbers, doc_count - 1)
    picked = jax.random.randint(pick_key, (SEQS // SEQS_DEV,), 0, SEQS_DEV)
    seq_rows = jnp.arange(SEQS, dtype=jnp.int32)
    single_doc = seq_rows % SEQS_DEV == picked[seq_rows // SEQS_DEV]
    numbers = jnp.where(single_doc[:, None], 0, numbers)
    return jnp.transpose(numbers).astype(jnp.int32)


def block_levels(rng, shape, pieces, low, largest):
    level, own = 1.0, jax.random.fold_in(rng, 6)
    for axis_at, blocks in pieces:
        heights = jnp.exp(jax.random.uniform(jax.random.fold_in(own, axis_at), (blocks,), jnp.float32, low / len(pieces), largest / len(pieces)))
        level = level * jnp.repeat(heights, shape[axis_at] // blocks).reshape([-1 if axis == axis_at else 1 for axis in range(len(shape))])
    return level


def noise(rng, shape, scale, limit, shards=(), kind=jnp.bfloat16):
    result = scale * jax.random.normal(rng, shape, jnp.float32)
    if shards:
        result = result * block_levels(rng, shape, shards, -0.22, 0.18)
    return jnp.clip(result, -limit, limit).astype(kind)


def setup_inputs(seed: int = 0) -> dict:
    key_list = jax.random.split(jax.random.key(seed), 16)
    return {
        "tokens": noise(key_list[0], (SEQ_LEN, SEQS, D), 1.0, 6.0, ((0, 4), (1, 2))),
        "segments": draw_segments(jax.random.fold_in(key_list[15], 71), 0),
        "ln1_gain": jnp.clip(1.0 + 0.1 * jax.random.normal(key_list[2], (D,), jnp.float32), 0.5, 1.5),
        "ln1_bias": noise(key_list[3], (D,), 0.2, 1.0, (), jnp.float32),
        "qkv_weight": noise(key_list[4], (D, 3, D), D ** -0.5, 0.21875, ((2, 4),)),
        "qv_bias": noise(key_list[5], (2, D), 0.2, 1.0, ((1, 4),), jnp.float32),
        "out_weight": noise(key_list[6], (D, D), (max(D // 64, 1)) ** -0.5, 1.75, ((0, 4),)),
        "out_bias": noise(key_list[7], (D,), 0.2, 1.0, (), jnp.float32),
        "ln2_gain": jnp.clip(1.0 + 0.1 * jax.random.normal(key_list[8], (D,), jnp.float32), 0.5, 1.5),
        "ln2_bias": noise(key_list[9], (D,), 0.2, 1.0, (), jnp.float32),
        "fc1_weight": noise(key_list[10], (D, FF), D ** -0.5, 0.21875, ((1, 4),)),
        "fc1_bias": noise(key_list[11], (FF,), 0.2, 1.0, ((0, 4),), jnp.float32),
        "fc2_weight": noise(key_list[12], (FF, D), FF ** -0.5, 0.109375, ((0, 4),)),
        "fc2_bias": noise(key_list[13], (D,), 0.2, 1.0, (), jnp.float32),
        "cotangent": noise(key_list[14], (SEQ_LEN, SEQS, D), 1.0, 6.0, ((0, 4), (1, 2))),
    }


masked_value = -1e+30
epsilon = 1e-05

@jax.custom_vjp
def low(v):
    return lax.optimization_barrier(v.astype(jnp.bfloat16)).astype(jnp.float32)

@jax.custom_vjp
def low_back(v):
    return v

def low_keep(v):
    return (low(v), None)

def low_pass(kept, grad):
    return (grad,)

def back_keep(v):
    return (v, None)

def back_low(kept, grad):
    return (low(grad),)
low.defvjp(low_keep, low_pass)
low_back.defvjp(back_keep, back_low)

def layer_norm(values_in, gain_vec, shift_vec):
    center = values_in - lax.optimization_barrier(jnp.mean(values_in, axis=-1, keepdims=True))
    spread = lax.optimization_barrier(jnp.mean(center * center, axis=-1, keepdims=True))
    return center * lax.rsqrt(spread + epsilon) * gain_vec + shift_vec

def attend(queries, keys, values, segments):
    length, seq_count, width_all = queries.shape
    head_count = width_all // HEAD_DIM
    block_rows = math.gcd(length, 512)
    positions = jnp.arange(length, dtype=jnp.int32)
    score_scale = HEAD_DIM ** (-0.5)

    def one_sequence(carried, seq_items):
        seq_queries, seq_keys, seq_values, seq_segments = seq_items
        key_heads = seq_keys.reshape(length, head_count, HEAD_DIM)
        value_heads = seq_values.reshape(length, head_count, HEAD_DIM)

        def one_block(block_items):
            block_queries, block_pos, block_seg = block_items
            scores = jnp.einsum('qhe,khe->hqk', block_queries, key_heads, precision=lax.Precision.HIGHEST) * score_scale
            allowed = (block_seg[:, None] == seq_segments[None, :]) & (positions[None, :] <= block_pos[:, None])
            scores = low_back(jnp.where(allowed[None], scores, masked_value))
            log_total = jax.nn.logsumexp(scores, axis=-1, keepdims=True)
            probs_low = low(jnp.exp(scores - log_total))
            return jnp.einsum('hqk,khe->qhe', probs_low, value_heads, precision=lax.Precision.HIGHEST)
        query_blocks = seq_queries.reshape(length // block_rows, block_rows, head_count, HEAD_DIM)
        attention_output = lax.map(jax.checkpoint(one_block), (query_blocks, positions.reshape(-1, block_rows), seq_segments.reshape(-1, block_rows)))
        return (carried, attention_output.reshape(length, width_all))
    carried, attention_output = lax.scan(one_sequence, jnp.zeros((), jnp.float32), (jnp.transpose(queries, (1, 0, 2)), jnp.transpose(keys, (1, 0, 2)), jnp.transpose(values, (1, 0, 2)), jnp.transpose(segments)))
    return jnp.transpose(attention_output, (1, 0, 2))

def reference(tokens, segments, ln1_gain, ln1_bias, qkv_weight, qv_bias, out_weight, out_bias, ln2_gain, ln2_bias, fc1_weight, fc1_bias, fc2_weight, fc2_bias, cotangent):

    def forward(inputs, gain_one, shift_one, qkv_mat, qv_shift, output_matrix, output_offset_bias, gain_two, shift_two, first_dense_matrix, first_dense_bias, second_dense_matrix, second_dense_bias):
        normed1 = low(layer_norm(inputs, gain_one, shift_one))
        projected = jnp.einsum('lsd,dtf->lstf', normed1, qkv_mat, precision=lax.Precision.HIGHEST)
        queries = low(low_back(projected[:, :, 0] + qv_shift[0]))
        keys = low(low_back(projected[:, :, 1]))
        values = low(low_back(projected[:, :, 2] + qv_shift[1]))
        attention_output = low(low_back(attend(queries, keys, values, segments)))
        residual_branch = low_back(jnp.einsum('mzx,xj->mzj', attention_output, output_matrix, precision=lax.Precision.HIGHEST)) + output_offset_bias
        residual_stream = inputs + residual_branch
        second_normed_input = low(layer_norm(residual_stream, gain_two, shift_two))
        hidden_preactivation = low_back(jnp.einsum('vqm,mh->vqh', second_normed_input, first_dense_matrix, precision=lax.Precision.HIGHEST) + first_dense_bias)
        hidden_activated = low(jax.nn.gelu(hidden_preactivation, approximate=True))
        return residual_stream + jnp.einsum('mzx,xj->mzj', hidden_activated, second_dense_matrix, precision=lax.Precision.HIGHEST) + second_dense_bias
    output, pullback = jax.vjp(forward, tokens.astype(jnp.float32), ln1_gain, ln1_bias, qkv_weight.astype(jnp.float32), qv_bias, out_weight.astype(jnp.float32), out_bias, ln2_gain, ln2_bias, fc1_weight.astype(jnp.float32), fc1_bias, fc2_weight.astype(jnp.float32), fc2_bias)
    gradients = pullback(cotangent.astype(jnp.float32))
    return (output.astype(jnp.bfloat16), gradients[0], gradients[1], gradients[2], gradients[3], gradients[4], gradients[5], gradients[6], gradients[7], gradients[8], gradients[9], gradients[10], gradients[11], gradients[12])
```

```python
import functools

import jax
import jax.numpy as jnp
from jax import lax
from jax.experimental import pallas as pl
from jax.experimental.pallas import tpu as pltpu
from jax.sharding import PartitionSpec as P

HEAD_DIM = 64


masked_value = -1e30
epsilon = 1e-05
vmem_bytes = 48 * 1024 * 1024
MESH = pl.DeviceIdType.MESH


def layer_norm(values_in, gain_vec, shift_vec):
    center = values_in - jnp.mean(values_in, axis=-1, keepdims=True)
    spread = jnp.mean(center * center, axis=-1, keepdims=True)
    return center * lax.rsqrt(spread + epsilon) * gain_vec + shift_vec


def smooth(values_in):
    return jax.nn.gelu(values_in, approximate=True)


def dot(left, right, left_dim, right_dim):
    return lax.dot_general(
        left, right, (((left_dim,), (right_dim,)), ((), ())), preferred_element_type=jnp.float32
    )


def masked_scores(key_rows, query_rows, doc_start, block_at, rows, diagonal):
    scores = dot(key_rows, query_rows, 0, 0)
    key_at = lax.broadcasted_iota(jnp.int32, (rows, rows), 0)
    allowed = key_at >= doc_start - block_at * rows
    if diagonal:
        allowed = allowed & (key_at <= lax.broadcasted_iota(jnp.int32, (rows, rows), 1))
    return jnp.where(allowed, scores, masked_value)


def forward_kernel(place_ref, query_ref, pair_ref, start_ref, out_ref, lse_ref, top_ref, total_ref):
    place = place_ref[0]
    width, rows = query_ref.shape[1], query_ref.shape[2]
    doc_start = start_ref[0]

    def block(block_at, diagonal):
        for head in range(width // HEAD_DIM):
            at = pl.ds(head * HEAD_DIM, HEAD_DIM)
            scores = masked_scores(
                pair_ref[block_at, 0, at, :], query_ref[0, at, :], doc_start, block_at, rows, diagonal
            )
            value_rows = pair_ref[block_at, 0, pl.ds(width + head * HEAD_DIM, HEAD_DIM), :]
            block_top = jnp.max(scores, axis=0, keepdims=True)
            line = pl.ds(head, 1)
            if diagonal:
                weights = jnp.exp(scores - block_top)
                top_ref[line, :] = block_top
                total_ref[line, :] = jnp.sum(weights, axis=0, keepdims=True)
                out_ref[0, at, :] = dot(value_rows, weights.astype(jnp.bfloat16), 1, 0)
            else:
                old_top = top_ref[line, :]
                new_top = jnp.maximum(old_top, block_top)
                weights = jnp.exp(scores - new_top)
                factor = jnp.exp(old_top - new_top)
                top_ref[line, :] = new_top
                total_ref[line, :] = total_ref[line, :] * factor + jnp.sum(
                    weights, axis=0, keepdims=True
                )
                out_ref[0, at, :] = out_ref[0, at, :] * factor + dot(
                    value_rows, weights.astype(jnp.bfloat16), 1, 0
                )

    block(place, True)

    @pl.loop(0, place)
    def others(block_at):
        block(block_at, False)

    for head in range(width // HEAD_DIM):
        at, line = pl.ds(head * HEAD_DIM, HEAD_DIM), pl.ds(head, 1)
        total = total_ref[line, :]
        out_ref[0, at, :] = out_ref[0, at, :] / total
        lse_ref[0, line, :] = top_ref[line, :] + jnp.log(total)


def backward_kernel(
    place_ref, query_ref, pair_ref, start_ref, out_ref, lse_ref, grad_ref, dq_ref, terms_ref, delta_ref
):
    place = place_ref[0]
    width, rows = query_ref.shape[1], query_ref.shape[2]
    blocks = pair_ref.shape[0]
    doc_start = start_ref[0]
    for head in range(width // HEAD_DIM):
        at = pl.ds(head * HEAD_DIM, HEAD_DIM)
        delta_ref[pl.ds(head, 1), :] = jnp.sum(
            grad_ref[0, at, :].astype(jnp.float32) * out_ref[0, at, :], axis=0, keepdims=True
        )

    def block(block_at, diagonal):
        for head in range(width // HEAD_DIM):
            at = pl.ds(head * HEAD_DIM, HEAD_DIM)
            value_at = pl.ds(width + head * HEAD_DIM, HEAD_DIM)
            line = pl.ds(head, 1)
            key_rows, query_rows = pair_ref[block_at, 0, at, :], query_ref[0, at, :]
            grad_rows = grad_ref[0, at, :]
            scores = masked_scores(key_rows, query_rows, doc_start, block_at, rows, diagonal)
            probs = jnp.exp(scores - lse_ref[0, line, :])
            grad_probs = dot(pair_ref[block_at, 0, value_at, :], grad_rows, 0, 0)
            grad_scores = (probs * (grad_probs - delta_ref[line, :])).astype(jnp.bfloat16)
            terms_ref[block_at, 0, value_at, :] = dot(
                grad_rows, probs.astype(jnp.bfloat16), 1, 1
            ).astype(jnp.bfloat16)
            terms_ref[block_at, 0, at, :] = dot(query_rows, grad_scores, 1, 1).astype(jnp.bfloat16)
            added = dot(key_rows, grad_scores, 1, 0) * (HEAD_DIM**-0.5)
            if diagonal:
                dq_ref[0, at, :] = added
            else:
                dq_ref[0, at, :] += added

    block(place, True)

    @pl.loop(0, place)
    def others(block_at):
        block(block_at, False)

    @pl.loop(place + 1, blocks)
    def later(block_at):
        terms_ref[block_at, 0] = jnp.zeros(terms_ref.shape[2:], terms_ref.dtype)


def sequence_spec(shape):
    return pl.BlockSpec((1,) + shape[1:], lambda seq, place: (seq, 0, 0))


def pair_spec(shape):
    return pl.BlockSpec((shape[0], 1) + shape[2:], lambda seq, place: (0, seq, 0, 0))


def attend(place, queries, pairs, starts):
    seqs, width, rows = queries.shape
    heads = width // HEAD_DIM
    work = seqs * width * rows * rows * pairs.shape[0]
    return pl.pallas_call(
        forward_kernel,
        out_shape=(
            jax.ShapeDtypeStruct(queries.shape, jnp.float32),
            jax.ShapeDtypeStruct((seqs, heads, rows), jnp.float32),
        ),
        grid_spec=pltpu.PrefetchScalarGridSpec(
            num_scalar_prefetch=1,
            grid=(seqs,),
            in_specs=[sequence_spec(queries.shape), pair_spec(pairs.shape), sequence_spec(starts.shape)],
            out_specs=[sequence_spec(queries.shape), sequence_spec((seqs, heads, rows))],
            scratch_shapes=[pltpu.VMEM((heads, rows), jnp.float32)] * 2,
        ),
        compiler_params=pltpu.CompilerParams(vmem_limit_bytes=vmem_bytes),
        cost_estimate=pl.CostEstimate(
            flops=4 * work, bytes_accessed=6 * 1024 * 1024, transcendentals=work // HEAD_DIM
        ),
    )(place, queries, pairs, starts)


def attend_back(place, queries, pairs, starts, attention, log_total, grads):
    seqs, width, rows = queries.shape
    heads = width // HEAD_DIM
    work = seqs * width * rows * rows * pairs.shape[0]
    tall = sequence_spec(queries.shape)
    return pl.pallas_call(
        backward_kernel,
        out_shape=(
            jax.ShapeDtypeStruct(queries.shape, jnp.float32),
            jax.ShapeDtypeStruct(pairs.shape, jnp.bfloat16),
        ),
        grid_spec=pltpu.PrefetchScalarGridSpec(
            num_scalar_prefetch=1,
            grid=(seqs,),
            in_specs=[
                tall,
                pair_spec(pairs.shape),
                sequence_spec(starts.shape),
                tall,
                sequence_spec(log_total.shape),
                tall,
            ],
            out_specs=[tall, pair_spec(pairs.shape)],
            scratch_shapes=[pltpu.VMEM((heads, rows), jnp.float32)],
        ),
        compiler_params=pltpu.CompilerParams(vmem_limit_bytes=vmem_bytes),
        cost_estimate=pl.CostEstimate(
            flops=10 * work, bytes_accessed=12 * 1024 * 1024, transcendentals=work // HEAD_DIM
        ),
    )(place, queries, pairs, starts, attention, log_total, grads)


def greet(count):
    me = lax.axis_index("tensor")
    barrier = pltpu.get_barrier_semaphore()
    for ahead in range(1, count):
        pl.semaphore_signal(
            barrier, inc=1, device_id={"tensor": lax.rem(me + ahead, count)}, device_id_type=MESH
        )
    pl.semaphore_wait(barrier, count - 1)
    return me


def gather_kernel(count, own_ref, all_ref, send_sem, recv_sem):
    me = greet(count)
    copies = []
    for ahead in range(1, count):
        copies.append(
            pltpu.make_async_remote_copy(
                src_ref=own_ref,
                dst_ref=all_ref.at[me],
                send_sem=send_sem.at[ahead - 1],
                recv_sem=recv_sem.at[ahead - 1],
                device_id={"tensor": lax.rem(me + ahead, count)},
                device_id_type=MESH,
            )
        )
        copies[-1].start()
    all_ref[me] = own_ref[...]
    for copy in copies:
        copy.wait()


def tensor_gather(own, count, collective_id):
    whole = pl.BlockSpec(memory_space=pltpu.VMEM)
    return pl.pallas_call(
        functools.partial(gather_kernel, count),
        out_shape=jax.ShapeDtypeStruct((count,) + own.shape, own.dtype),
        in_specs=[whole],
        out_specs=whole,
        scratch_shapes=[pltpu.SemaphoreType.DMA((count - 1,))] * 2,
        compiler_params=pltpu.CompilerParams(
            collective_id=collective_id, has_side_effects=True, vmem_limit_bytes=vmem_bytes
        ),
    )(own)


def sum_kernel(count, pieces, part_ref, out_ref, inbox, send_sem, recv_sem):
    me = greet(count)
    rows = part_ref.shape[1] // pieces

    def copy(phase, piece, ahead):
        peer = lax.rem(me + ahead, count)
        at = pl.ds(piece * rows, rows)
        if phase == 0:
            source, target = part_ref.at[peer, at], inbox.at[ahead - 1, at]
        else:
            source, target = out_ref.at[me, at], out_ref.at[me, at]
        return pltpu.make_async_remote_copy(
            src_ref=source,
            dst_ref=target,
            send_sem=send_sem.at[phase, piece, ahead - 1],
            recv_sem=recv_sem.at[phase, piece, ahead - 1],
            device_id={"tensor": peer},
            device_id_type=MESH,
        )

    for piece in range(pieces):
        for ahead in range(1, count):
            copy(0, piece, ahead).start()
    for piece in range(pieces):
        at = pl.ds(piece * rows, rows)
        total = part_ref[me, at, :].astype(jnp.float32)
        for ahead in range(1, count):
            copy(0, piece, ahead).wait_recv()
            total = total + inbox[ahead - 1, at, :].astype(jnp.float32)
        out_ref[me, at, :] = total.astype(out_ref.dtype)
        for ahead in range(1, count):
            copy(1, piece, ahead).start()
    for piece in range(pieces):
        for ahead in range(1, count):
            copy(0, piece, ahead).wait_send()
            copy(1, piece, ahead).wait()


def tensor_sum(part, count):
    pieces = 2
    low = part.astype(jnp.bfloat16).reshape(count, -1, part.shape[-1])
    whole = pl.BlockSpec(memory_space=pltpu.VMEM)
    summed = pl.pallas_call(
        functools.partial(sum_kernel, count, pieces),
        out_shape=jax.ShapeDtypeStruct(low.shape, low.dtype),
        in_specs=[whole],
        out_specs=whole,
        scratch_shapes=[pltpu.VMEM((count - 1,) + low.shape[1:], low.dtype)]
        + [pltpu.SemaphoreType.DMA((2, pieces, count - 1))] * 2,
        compiler_params=pltpu.CompilerParams(
            collective_id=1, has_side_effects=True, vmem_limit_bytes=vmem_bytes
        ),
        cost_estimate=pl.CostEstimate(
            flops=low.size * 40, bytes_accessed=64 * 1024 * 1024, transcendentals=0
        ),
    )(low)
    return summed.reshape(part.shape).astype(jnp.float32)


def on_device(
    tensors,
    tokens,
    segments,
    ln1_gain,
    ln1_bias,
    qkv_weight,
    qv_bias,
    out_weight,
    out_bias,
    ln2_gain,
    ln2_bias,
    fc1_weight,
    fc1_bias,
    fc2_weight,
    fc2_bias,
    cotangent,
):
    ctx_rows, seqs_local = (tokens.shape[0], tokens.shape[1])
    local_width = qkv_weight.shape[2]
    block_at = lax.axis_index("context")
    first_row = block_at * ctx_rows
    place = jnp.reshape(block_at, (1,)).astype(jnp.int32)
    by_sequence = jnp.transpose(segments)
    own_segments = lax.dynamic_slice_in_dim(by_sequence, first_row, ctx_rows, 1)
    starts = jnp.sum(
        (by_sequence[:, None, :] < own_segments[:, :, None]).astype(jnp.int32), axis=-1
    )[:, None, :]
    inputs = jnp.transpose(tokens, (1, 0, 2)).astype(jnp.float32)
    normed1, ln1_pull = jax.vjp(layer_norm, inputs, ln1_gain, ln1_bias)
    acts_one = normed1.astype(jnp.bfloat16)
    projected = jnp.einsum(
        "scd,dtf->stfc", acts_one, qkv_weight, preferred_element_type=jnp.float32
    )
    queries = (projected[:, 0] + qv_bias[0][None, :, None]).astype(jnp.bfloat16)
    queries = queries * jnp.bfloat16(HEAD_DIM**-0.5)
    key_vals = jnp.concatenate(
        [projected[:, 1], projected[:, 2] + qv_bias[1][None, :, None]], axis=1
    ).astype(jnp.bfloat16)
    pairs = lax.all_gather(key_vals, "context", axis=0)
    out_whole = tensor_gather(out_weight, tensors, 3)
    attention, log_total = attend(place, queries, pairs, starts)
    attn_low = attention.astype(jnp.bfloat16)
    attn_whole = tensor_gather(attn_low, tensors, 2)
    branch = jnp.einsum("tsfc,tfd->scd", attn_whole, out_whole, preferred_element_type=jnp.float32)
    residual_stream = inputs + branch + out_bias
    second_normed_input, ln2_pull = jax.vjp(layer_norm, residual_stream, ln2_gain, ln2_bias)
    acts_two = second_normed_input.astype(jnp.bfloat16)
    hidden_preactivation = (
        jnp.einsum("scd,df->scf", acts_two, fc1_weight, preferred_element_type=jnp.float32)
        + fc1_bias
    )
    hidden_activated, smooth_pull = jax.vjp(smooth, hidden_preactivation)
    hidden_low = hidden_activated.astype(jnp.bfloat16)
    mlp_part = jnp.einsum("scf,fd->scd", hidden_low, fc2_weight, preferred_element_type=jnp.float32)
    grad_in = jnp.transpose(cotangent, (1, 0, 2))
    grad_out = grad_in.astype(jnp.float32)
    grad_hidden = jnp.einsum(
        "scd,fd->scf", grad_in, fc2_weight, preferred_element_type=jnp.float32
    )
    grad_pre = smooth_pull(grad_hidden)[0].astype(jnp.bfloat16)
    mlp_back = jnp.einsum("scf,df->scd", grad_pre, fc1_weight, preferred_element_type=jnp.float32)
    fc2_weight_grad = jnp.einsum(
        "scf,scd->fd", hidden_low, grad_in, preferred_element_type=jnp.float32
    )
    fc2_bias_grad = jnp.sum(grad_out, axis=(0, 1))
    fc1_bias_grad = jnp.sum(grad_pre.astype(jnp.float32), axis=(0, 1))
    fc1_weight_grad = jnp.einsum(
        "scd,scf->df", acts_two, grad_pre, preferred_element_type=jnp.float32
    )
    dense = jnp.stack([fc1_weight_grad.astype(jnp.bfloat16), fc2_weight_grad.astype(jnp.bfloat16)])
    grad_normed2 = tensor_sum(mlp_back, tensors)
    resid_from_norm, ln2_gain_grad, ln2_bias_grad = ln2_pull(grad_normed2)
    grad_resid = grad_out + resid_from_norm
    grad_branch = grad_resid.astype(jnp.bfloat16)
    out_weight_grad = jnp.einsum(
        "sfc,scd->fd", attn_low, grad_branch, preferred_element_type=jnp.float32
    )
    out_bias_grad = jnp.sum(grad_resid, axis=(0, 1))
    grad_attn = jnp.einsum(
        "scd,fd->sfc", grad_branch, out_weight, preferred_element_type=jnp.float32
    ).astype(jnp.bfloat16)
    grad_query, terms = attend_back(place, queries, pairs, starts, attention, log_total, grad_attn)
    mlp_low, terms = lax.optimization_barrier((mlp_part.astype(jnp.bfloat16), terms))
    key_grads = lax.psum_scatter(terms, "context", scatter_dimension=0)
    mlp_total = tensor_sum(mlp_low, tensors)
    output = (residual_stream + mlp_total + fc2_bias).astype(jnp.bfloat16)
    query_grad_low = grad_query.astype(jnp.bfloat16)
    stacked = jnp.concatenate([query_grad_low, key_grads], axis=1).reshape(
        seqs_local, 3, local_width, ctx_rows
    )
    qkv_back = jnp.einsum("stfc,dtf->scd", stacked, qkv_weight, preferred_element_type=jnp.float32)
    ln1_gain_part, ln1_bias_part = ln1_pull(qkv_back)[1:]
    qkv_weight_grad = jnp.einsum(
        "scd,stfc->dtf", acts_one, stacked, preferred_element_type=jnp.float32
    )
    bias_sums = jnp.sum(stacked.astype(jnp.float32), axis=(0, 3))
    thin = jnp.concatenate([fc1_bias_grad, bias_sums[0], bias_sums[2]])
    hidden_local, model_width = fc1_bias.shape[0], tokens.shape[2]
    thin_rows = pl.cdiv(thin.shape[0], model_width)
    packed = jnp.concatenate(
        [
            out_weight_grad,
            jnp.stack(
                [ln1_gain_part, ln1_bias_part, out_bias_grad, ln2_gain_grad, ln2_bias_grad, fc2_bias_grad]
            ),
            jnp.pad(thin, (0, thin_rows * model_width - thin.shape[0])).reshape(thin_rows, -1),
        ]
    )
    packed, qkv_low, qkv_back = lax.optimization_barrier(
        (packed.astype(jnp.bfloat16), qkv_weight_grad.astype(jnp.bfloat16), qkv_back)
    )
    dense, packed, qkv_sum = lax.psum((dense, packed, qkv_low), ("dp", "context"))
    grad_normed1, dense, packed, qkv_sum = lax.optimization_barrier(
        (tensor_sum(qkv_back, tensors), dense, packed, qkv_sum)
    )
    inputs_from_norm = ln1_pull(grad_normed1)[0]
    grad_tokens = grad_resid + inputs_from_norm
    packed = packed.astype(jnp.float32)
    lines = packed[local_width : local_width + 6]
    ln1_sums = jnp.sum(tensor_gather(lines[:2], tensors, 4), axis=0)
    thin = packed[local_width + 6 :].reshape(-1)[: thin.shape[0]]
    return (
        jnp.transpose(output, (1, 0, 2)),
        jnp.transpose(grad_tokens, (1, 0, 2)),
        ln1_sums[0],
        ln1_sums[1],
        qkv_sum.astype(jnp.float32),
        thin[hidden_local:].reshape(2, local_width),
        packed[:local_width],
        lines[2],
        lines[3],
        lines[4],
        dense[0].astype(jnp.float32),
        thin[:hidden_local],
        dense[1].astype(jnp.float32),
        lines[5],
    )


def solution(mesh):
    placed = (
        P("context", "dp", None),
        P(None, "dp"),
        P(),
        P(),
        P(None, None, "tensor"),
        P(None, "tensor"),
        P("tensor", None),
        P(),
        P(),
        P(),
        P(None, "tensor"),
        P("tensor"),
        P("tensor", None),
        P(),
        P("context", "dp", None),
    )
    return jax.shard_map(
        functools.partial(on_device, mesh.shape["tensor"]),
        mesh=mesh,
        in_specs=placed,
        out_specs=(
            P("context", "dp", None),
            P("context", "dp", None),
            P(),
            P(),
            P(None, None, "tensor"),
            P(None, "tensor"),
            P("tensor", None),
            P(),
            P(),
            P(),
            P(None, "tensor"),
            P("tensor"),
            P("tensor", None),
            P(),
        ),
        check_vma=False,
    )
```
